512 devices in a mesh: tm: 16 (over y_lo, x, core), mp: 8 (over z), dp: 4 (over y_hi).
Axes of the slice: x: 4, y: 8 (y_hi: 4, y_lo: 2; y = y_hi * 2 + y_lo), z: 8, core: 2. Of those that a mesh axis runs over, the one named last changes fastest.
Arguments:
- q_proj: bfloat16 [4, 6144, 5120], P('dp', 'tm', 'mp'), may hold values from -80 to 80
- k_proj: bfloat16 [4, 6144, 5120], P('dp', 'tm', 'mp'), may hold values from -80 to 80
- values: bfloat16 [4, 6144, 5120], P('dp', 'tm', 'mp'), may hold values from -6 to 6
- grad_out: bfloat16 [4, 6144, 5120], P('dp', 'tm', 'mp'), may hold values from -48 to 48
- gain_q: float32 [5120], P('mp'), may hold values from 0.5 to 1.5
- gain_k: float32 [5120], P('mp'), may hold values from 0.5 to 1.5
- valid_count: int32 [4, 16], P('dp', 'tm'), may hold values from 192 to 384, as said below
- segment: int32 [4, 16], P('dp', 'tm'), may hold values from 0 to 3, never falling along the last dimension, each value on 1 to 8 neighbouring positions
Outputs:
- query_grad: bfloat16 [4, 6144, 5120], P('dp', 'tm', 'mp')
- key_grad: bfloat16 [4, 6144, 5120], P('dp', 'tm', 'mp')
- value_grad: bfloat16 [4, 6144, 5120], P('dp', 'tm', 'mp')
- gain_q_grad: float32 [5120], P('mp')
- gain_k_grad: float32 [5120], P('mp')
The draws below stay inside these ranges and needn't reach their ends.
Inputs may be any that keep to these rules, and one draw needn't show every extreme that they name: `valid_count`: the valid tokens of a group are its first slots; some group is full. `segment`: along a rollout the scene ids never fall, start at 0 and skip none; a scene spans at most 8 groups.
All inputs are finite; a program needn't handle non-finite values.
Results may differ from the reference program's by a relative error of at most 0.011.
Values may be sent and summed in bfloat16 or wider, within the bound.
No kernel may reach another device: no remote copies, remote signals or barrier semaphores. Data moves between devices by JAX's collectives and lax.ppermute only.
A program may use at most 64 MiB of HBM per device.

```python
import math
import jax
import jax.numpy as jnp
import numpy as np
from jax import lax

HEADS = 40
HD = 128
D = 5120
C = 384
WIN = 3
NCHUNK = 16
TOKENS = 6144
ROLLS = 4


def ramp_factor(length, spread):
    position = jnp.arange(length, dtype=jnp.float32) / max(length - 1, 1)
    return jnp.exp(jnp.log(spread) * (position - 0.5))


def rough_factor(subkey, full_shape):
    return jnp.exp(jax.random.uniform(subkey, full_shape, jnp.float32, -1.15, 1.15))


def scaled_rows(core_draw, subkey):
    subkeys = jax.random.split(subkey, 2)
    column = ramp_factor(D, 3.0) * rough_factor(subkeys[0], (D,))
    row_scale = rough_factor(subkeys[1], (ROLLS * TOKENS, 1))
    return core_draw * column[None, :] * row_scale


def draw_q_proj(key, part):
    own_key = jax.random.fold_in(key, 101)
    subkeys = jax.random.split(own_key, 2)
    full_shape = (ROLLS * TOKENS, D)
    core_draw = jnp.clip(jax.random.normal(subkeys[0], full_shape, jnp.float32), -4.0, 4.0)
    drawn = scaled_rows(core_draw, subkeys[1])
    return drawn.reshape(ROLLS, TOKENS, D).astype(jnp.bfloat16)


def draw_k_proj(key, part):
    own_key = jax.random.fold_in(key, 202)
    subkeys = jax.random.split(own_key, 2)
    full_shape = (ROLLS * TOKENS, D)
    core_draw = jnp.clip(jax.random.normal(subkeys[0], full_shape, jnp.float32), -4.0, 4.0)
    drawn = scaled_rows(core_draw, subkeys[1])
    return drawn.reshape(ROLLS, TOKENS, D).astype(jnp.bfloat16)


def draw_grad_out(key, part):
    own_key = jax.random.fold_in(key, 303)
    subkeys = jax.random.split(own_key, 2)
    full_shape = (ROLLS, NCHUNK, C, D)
    position = (jnp.arange(NCHUNK, dtype=jnp.float32)[None, :] + jnp.arange(ROLLS, dtype=jnp.float32)[:, None] / ROLLS) / NCHUNK
    row_scale = rough_factor(subkeys[1], (ROLLS, NCHUNK, C, 1))
    core_draw = jnp.clip(jax.random.normal(subkeys[0], full_shape, jnp.float32), -4.0, 4.0)
    slope = jnp.exp(jnp.log(3.0) * (position - 0.5))
    drawn = core_draw * row_scale * slope[:, :, None, None]
    return jnp.clip(drawn, -48.0, 48.0).reshape(ROLLS, TOKENS, D).astype(jnp.bfloat16)


def draw_valid_count(key, part):
    own_key = jax.random.fold_in(key, 404)
    subkeys = jax.random.split(own_key, 2)
    counts = jax.random.randint(subkeys[0], (ROLLS, NCHUNK), C // 2, C + 1, jnp.int32)
    full_at = jax.random.randint(subkeys[1], (), 0, ROLLS * NCHUNK, jnp.int32)
    flat_index = jnp.arange(ROLLS * NCHUNK, dtype=jnp.int32).reshape(ROLLS, NCHUNK)
    return jnp.where(flat_index == full_at, C, counts).astype(jnp.int32)


def block_scale(key, extent, cuts, smallest, largest):
    level = 1.0
    for dim, parts in cuts:
        draws = jax.random.uniform(jax.random.fold_in(jax.random.fold_in(key, 6), dim), (parts,), jnp.float32, smallest / len(cuts), largest / len(cuts))
        level = level * jnp.repeat(jnp.exp(draws), extent[dim] // parts).reshape((-1,) + (1,) * (len(extent) - 1 - dim))
    return level


def length_profile(amount, total, limit, skew):
    weights = [(1 << 20) // math.isqrt(grade ** skew) + 1 for grade in range(2, amount + 1)]
    spare, given = total - limit - (amount - 1), [1] * (amount - 1)
    while spare > 0:
        movable = [i for i in range(amount - 1) if given[i] < limit]
        pool, budget = sum([weights[i] for i in movable]), spare
        for i in movable:
            extra = min(limit - given[i], max(1, budget * weights[i] // pool), spare)
            given[i] = given[i] + extra
            spare = spare - extra
    return np.array([limit] + given)


def ragged(key, number_of, total, limit, skew):
    if number_of == 2:
        one = jax.random.randint(key, (), max(1, total - limit), min(limit, total - 1) + 1)
        return jnp.stack([one, total - one])
    tallies = jnp.asarray(length_profile(number_of, total, limit, skew), jnp.int32)
    twos = (number_of - 1) // 2
    donor, sink = tallies[1:1 + 2 * twos:2], tallies[2:2 + 2 * twos:2]
    room = jnp.minimum(donor - 1, limit - sink)
    shifted = jax.random.randint(jax.random.fold_in(key, 1), (twos,), 0, 1 << 20) % (room + 1)
    tallies = tallies.at[1:1 + 2 * twos:2].set(donor - shifted).at[2:2 + 2 * twos:2].set(sink + shifted)
    return tallies[jax.random.permutation(jax.random.fold_in(key, 2), number_of)]


def centred(stream_key, dims, deviation, bound, cuts=(), held_as=jnp.bfloat16):
    values = deviation * jax.random.normal(stream_key, dims, jnp.float32)
    if cuts:
        values = values * block_scale(stream_key, dims, cuts, -0.22, 0.18)
    return jnp.clip(values, -bound, bound).astype(held_as)


def setup_inputs(seed: int = 0) -> dict:
    streams_of = jax.random.split(jax.random.key(seed), 9)
    q_proj = draw_q_proj(jax.random.fold_in(streams_of[8], 71), 0)
    k_proj = draw_k_proj(jax.random.fold_in(streams_of[8], 71), 0)
    values = centred(streams_of[2], (ROLLS, TOKENS, D), 1.0, 6.0, ((0, 4), (1, 16), (2, 8)))
    grad_out = draw_grad_out(jax.random.fold_in(streams_of[8], 71), 0)
    gain_q = jnp.clip(1.0 + 0.1 * jax.random.normal(streams_of[4], (D,), jnp.float32), 0.5, 1.5)
    gain_k = jnp.clip(1.0 + 0.1 * jax.random.normal(streams_of[5], (D,), jnp.float32), 0.5, 1.5)
    valid_count = draw_valid_count(jax.random.fold_in(streams_of[8], 71), 0)
    segment = jax.vmap(lambda own: jnp.searchsorted(jnp.cumsum(ragged(own, max(2, NCHUNK // 4), NCHUNK, NCHUNK // 2, 0)), jnp.arange(NCHUNK), side="right"))(jax.random.split(streams_of[7], ROLLS)).reshape((ROLLS, NCHUNK)).astype(jnp.int32)
    return {"q_proj": q_proj, "k_proj": k_proj, "values": values, "grad_out": grad_out, "gain_q": gain_q, "gain_k": gain_k, "valid_count": valid_count, "segment": segment}


EPSILON = 1e-06
HIGHEST = lax.Precision.HIGHEST

def normed(raw_rows, gain_vec):
    widened = raw_rows.astype(jnp.float32)
    row_root = jnp.sqrt(lax.optimization_barrier(jnp.sum(widened * widened, axis=-1, keepdims=True)) / (HEADS * HD) + EPSILON)
    unit_rows = widened / row_root
    return (unit_rows, row_root, (unit_rows * gain_vec).astype(jnp.bfloat16))

def norm_back(unit_rows, row_root, gain_vec, grad_rows):
    scaled = grad_rows * gain_vec
    inner_sum = lax.optimization_barrier(jnp.sum(scaled * unit_rows, axis=-1, keepdims=True)) / (HEADS * HD)
    result = ((scaled - unit_rows * inner_sum) / row_root).astype(jnp.bfloat16)
    return (result, lax.optimization_barrier(jnp.sum(grad_rows * unit_rows, axis=0)))

def to_heads(new_block, row_count):
    return new_block.reshape(row_count, HEADS, HD).astype(jnp.float32)

def one_rollout(q_proj, k_proj, values, grad_out, valid_count, segment, gain_q, gain_k):
    full_width = HEADS * HD
    q_unit, q_root, q_norm = normed(q_proj, gain_q)
    k_unit, k_root, k_norm = normed(k_proj, gain_k)
    group_of = jnp.arange(NCHUNK * C, dtype=jnp.int32) // C
    slot_of = jnp.arange(NCHUNK * C, dtype=jnp.int32) % C
    is_live = slot_of < valid_count[group_of]
    grad_live = jnp.where(is_live[:, None], grad_out, jnp.zeros_like(grad_out))
    margin = WIN * C
    window_rows = margin + C
    k_pad = jnp.concatenate([jnp.zeros((margin, full_width), jnp.bfloat16), k_norm], axis=0)
    v_pad = jnp.concatenate([jnp.zeros((margin, full_width), jnp.bfloat16), values], axis=0)
    key_tag = jnp.where(is_live, segment[group_of] + 1, 0).astype(jnp.int32)
    tag_pad = jnp.concatenate([jnp.zeros((margin,), jnp.int32), key_tag], axis=0)
    root_size = math.sqrt(HD)

    def group_step(carried, group_index):
        k_total, v_total = carried
        row_start = (group_index * C).astype(jnp.int32)
        q_block = to_heads(lax.dynamic_slice_in_dim(q_norm, row_start, C, 0), C)
        g_block = to_heads(lax.dynamic_slice_in_dim(grad_live, row_start, C, 0), C)
        k_block = to_heads(lax.dynamic_slice_in_dim(k_pad, row_start, window_rows, 0), window_rows)
        v_block = to_heads(lax.dynamic_slice_in_dim(v_pad, row_start, window_rows, 0), window_rows)
        allowed = lax.dynamic_slice_in_dim(tag_pad, row_start, window_rows, 0) == segment[group_index] + 1
        scores = jnp.einsum('qhd,khd->hqk', q_block, k_block, precision=HIGHEST) / root_size
        scores = jnp.where(allowed[None, None, :], scores, -jnp.inf)
        row_max = lax.optimization_barrier(jnp.max(scores, axis=-1, keepdims=True))
        exponent = jnp.exp(scores - row_max)
        weights = exponent / lax.optimization_barrier(jnp.sum(exponent, axis=-1, keepdims=True))
        weights_low = lax.optimization_barrier(weights.astype(jnp.bfloat16)).astype(jnp.float32)
        grad_weights = jnp.einsum('qhd,khd->hqk', g_block, v_block, precision=HIGHEST)
        row_delta = lax.optimization_barrier(jnp.sum(weights * grad_weights, axis=-1, keepdims=True))
        grad_scores = lax.optimization_barrier((weights * (grad_weights - row_delta)).astype(jnp.bfloat16)).astype(jnp.float32)
        q_grad = jnp.einsum('hqk,khd->qhd', grad_scores, k_block, precision=HIGHEST) / root_size
        k_grad = jnp.einsum('hqk,qhd->khd', grad_scores, q_block, precision=HIGHEST) / root_size
        v_grad = jnp.einsum('hqk,qhd->khd', weights_low, g_block, precision=HIGHEST)
        k_old = lax.dynamic_slice_in_dim(k_total, row_start, window_rows, 0)
        v_old = lax.dynamic_slice_in_dim(v_total, row_start, window_rows, 0)
        k_total = lax.dynamic_update_slice_in_dim(k_total, k_old + k_grad.reshape(window_rows, full_width), row_start, 0)
        v_total = lax.dynamic_update_slice_in_dim(v_total, v_old + v_grad.reshape(window_rows, full_width), row_start, 0)
        return ((k_total, v_total), q_grad.reshape(C, full_width))
    initial = (jnp.zeros((margin + NCHUNK * C, full_width), jnp.float32), jnp.zeros((margin + NCHUNK * C, full_width), jnp.float32))
    (k_total, v_total), q_grads = lax.scan(group_step, initial, jnp.arange(NCHUNK, dtype=jnp.int32))
    q_grads = q_grads.reshape(NCHUNK * C, full_width)
    query_grad, gain_q_term = norm_back(q_unit, q_root, gain_q, q_grads)
    key_grad, gain_k_term = norm_back(k_unit, k_root, gain_k, k_total[margin:])
    return (query_grad, key_grad, v_total[margin:].astype(jnp.bfloat16), gain_q_term, gain_k_term)

def reference(q_proj, k_proj, values, grad_out, gain_q, gain_k, valid_count, segment):

    def per_rollout(pieces):
        return one_rollout(pieces[0], pieces[1], pieces[2], pieces[3], pieces[4], pieces[5], gain_q, gain_k)
    query_grad, key_grad, value_grad, gain_q_terms, gain_k_terms = lax.map(per_rollout, (q_proj, k_proj, values, grad_out, valid_count, segment))
    return (query_grad, key_grad, value_grad, lax.optimization_barrier(jnp.sum(gain_q_terms, axis=0)), lax.optimization_barrier(jnp.sum(gain_k_terms, axis=0)))
```

```python
import functools
import math

import jax
import jax.numpy as jnp
from jax import lax
from jax.experimental import pallas as pl
from jax.experimental.pallas import tpu as pltpu
from jax.sharding import PartitionSpec as P

HD = 128
EPSILON = 1e-06
MASKED = -1e30
CHUNKS = ((0, 2), (2, 5))
STRIP = 48
F32, LOW = jnp.float32, jnp.bfloat16
VMEM_LIMIT = 60 * 1024 * 1024


def along_lanes(row, width):
    return jnp.transpose(jnp.broadcast_to(row, (width, row.shape[1])))


def row_sums(block):
    return jnp.sum(jnp.transpose(block), axis=0, keepdims=True)


def folded(block, op):
    return functools.reduce(op, [block[at : at + 8] for at in range(0, block.shape[0], 8)])


def prepare_kernel(q_ref, k_ref, v_ref, own_out, power_out, total):
    slots = q_ref.shape[1]
    own_out[:slots, :] = k_ref[0]
    own_out[slots:, :] = v_ref[0]

    @pl.when(pl.program_id(0) == 0)
    def _():
        total[...] = jnp.zeros_like(total)

    for place, ref in enumerate((q_ref, k_ref)):
        part = ref[0].astype(F32)
        total[place] += part * part

    @pl.when(pl.program_id(0) == pl.num_programs(0) - 1)
    def _():
        for place in range(2):
            row = row_sums(total[place])
            for device in range(power_out.shape[0]):
                power_out[device, :, place * slots : (place + 1) * slots] = row


def roots_kernel(full_width, tag_ref, power_ref, note_out, q_out):
    slots = q_out.shape[1]
    power = power_ref[0]
    for device in range(1, power_ref.shape[0]):
        power += power_ref[device]
    inverse = 1.0 / jnp.sqrt(power / full_width + EPSILON)
    q_out[...] = inverse[:, :slots]
    lane = lax.broadcasted_iota(jnp.int32, (1, HD), 1)
    valid = tag_ref[1].astype(F32)
    segment = tag_ref[2].astype(F32)
    tags = jnp.where(lane == 0, valid, jnp.where(lane == 1, segment, 0.0))
    for device in range(note_out.shape[0]):
        note_out[device, :, :slots] = inverse[:, slots:]
        note_out[device, :, slots:] = tags


def head_kernel(
    first, total_heads, tag_ref, notes, q_inverse, gain_q_ref, gain_k_ref, q_ref, g_ref,
    own_ref, near_ref, side_ref, swap_ref, state_in,
    q_out, own_out, near_out, side_out, swap_out, state_out, rows_out,
    score_ref, grad_ref, weight_low, grad_low,
):
    step = pl.program_id(0)
    slots = q_ref.shape[1]
    width = total_heads * HD
    scale = 1.0 / math.sqrt(HD)
    mine = tag_ref[0]
    even = lax.rem(mine, 2) == 0
    distances = (0, 2, jnp.where(even, 3, 1), jnp.where(even, 1, 3))
    gain_q = gain_q_ref[...]
    gain_k = gain_k_ref[...]
    segment = tag_ref[2].astype(F32)
    q_unit = q_ref[0].astype(F32) * along_lanes(q_inverse[...], HD)
    q_norm = (q_unit * gain_q).astype(LOW)
    live = lax.broadcasted_iota(jnp.int32, (slots, HD), 0) < tag_ref[1]
    g_live = jnp.where(live, g_ref[0].astype(F32), 0.0).astype(LOW)
    q_side = jnp.transpose(q_norm)
    g_side = jnp.transpose(g_live)
    lanes = lax.broadcasted_iota(jnp.int32, (STRIP, slots), 0).astype(F32)
    refs = (own_ref, near_ref, side_ref, swap_ref)
    inverses, k_norms, limits = [], [], []
    for slot, ref in enumerate(refs):
        other = mine - distances[slot]
        at = jnp.maximum(other, 0)
        inverse = along_lanes(notes[at, :, :slots], HD)
        tags = notes[at, :, slots:]
        same = (tags[:, 1:2] == segment) & (other >= 0)
        limits.append(jnp.where(same, tags[:, 0:1], 0.0))
        k_norm = (ref[:slots, :].astype(F32) * inverse * gain_k).astype(LOW)
        inverses.append(inverse)
        k_norms.append(k_norm)
        rows = slice(slot * slots, (slot + 1) * slots)
        score_ref[rows, :] = jnp.dot(k_norm, q_side, preferred_element_type=F32)
        grad_ref[rows, :] = jnp.dot(ref[slots:, :], g_side, preferred_element_type=F32)
    strips = [(slot, at) for slot in range(4) for at in range(0, slots, STRIP)]
    top = jnp.full((8, slots), MASKED, F32)
    for slot, at in strips:
        base = slot * slots + at
        included = lanes < limits[slot] - at
        score = jnp.where(included, score_ref[base : base + STRIP, :], MASKED)
        top = jnp.maximum(top, folded(score, jnp.maximum))
    top = jnp.max(top, axis=0, keepdims=True)
    total = jnp.zeros((8, slots), F32)
    delta = jnp.zeros((8, slots), F32)
    for slot, at in strips:
        base = slot * slots + at
        included = lanes < limits[slot] - at
        score = jnp.where(included, score_ref[base : base + STRIP, :], MASKED)
        exponent = jnp.exp((score - top) * scale)
        score_ref[base : base + STRIP, :] = exponent
        total += folded(exponent, jnp.add)
        delta += folded(exponent * grad_ref[base : base + STRIP, :], jnp.add)
    inverse_sum = 1.0 / jnp.sum(total, axis=0, keepdims=True)
    delta = jnp.sum(delta, axis=0, keepdims=True) * inverse_sum
    q_turned = jnp.zeros((HD, slots), F32)
    k_gain = jnp.zeros((1, HD), F32)
    inners = []
    for slot, out in enumerate((own_out, near_out, side_out, swap_out)):
        for at in range(0, slots, STRIP):
            rows = slice(slot * slots + at, slot * slots + at + STRIP)
            weight = score_ref[rows, :] * inverse_sum
            weight_low[rows, :] = weight.astype(LOW)
            grad_low[rows, :] = (weight * (grad_ref[rows, :] - delta)).astype(LOW)
        rows = slice(slot * slots, (slot + 1) * slots)
        q_turned += jnp.dot(
            jnp.transpose(k_norms[slot]), grad_low[rows, :], preferred_element_type=F32
        )
        k_part = jnp.dot(grad_low[rows, :], q_norm, preferred_element_type=F32) * scale
        v_part = jnp.dot(weight_low[rows, :], g_live, preferred_element_type=F32)
        out[:slots, :] = k_part.astype(out.dtype)
        out[slots:, :] = v_part.astype(out.dtype)
        product = k_part * (refs[slot][:slots, :].astype(F32) * inverses[slot])
        k_gain += jnp.sum(product, axis=0, keepdims=True)
        inners.append(row_sums(product * gain_k))
    q_part = jnp.transpose(q_turned) * scale
    q_out[...] = q_part
    product = q_part * q_unit
    inners.append(row_sums(product * gain_q))

    @pl.when(step == 0)
    def _():
        state_out[...] = state_in[...]

    for slot, inner in enumerate(inners):
        state_out[slot : slot + 1, :slots] += inner
    at = (first + step) * HD
    state_out[5:6, pl.ds(pl.multiple_of(at, HD), HD)] = jnp.sum(product, axis=0, keepdims=True)
    state_out[5:6, pl.ds(pl.multiple_of(width + at, HD), HD)] = k_gain

    @pl.when(first + step == total_heads - 1)
    def _():
        for device in range(rows_out.shape[0]):
            rows_out[device, :, :slots] = jnp.zeros((1, slots), F32)
            rows_out[device, :, slots:] = state_out[5:6, :]
        for slot, distance in enumerate(distances):
            @pl.when(mine >= distance)
            def _():
                rows_out[mine - distance, :, :slots] = state_out[slot : slot + 1, :slots]


def collect_kernel(state_ref, rows_ref, out):
    slots = rows_ref.shape[2] - state_ref.shape[1]
    total = rows_ref[0]
    for device in range(1, rows_ref.shape[0]):
        total += rows_ref[device]
    for device in range(out.shape[0]):
        out[device, :, :slots] = state_ref[4:5, :slots]
        out[device, :, slots:] = total


def finish_kernel(
    full_width, sizes, tag_ref, notes, q_inverse, gain_q_ref, gain_k_ref, sums, q_ref, k_ref,
    q_part, own_part, side_back, near_back, *rest,
):
    query_out, key_out, value_out, gain_out = rest[-4:]
    slots = q_ref.shape[1]
    mine, mp, dp = tag_ref[0], tag_ref[3], tag_ref[4]
    mp_size, dp_size = sizes
    inner = sums[dp, :, : 2 * slots]
    for other in range(1, mp_size):
        inner += sums[other * dp_size + dp, :, : 2 * slots]
    inner = inner / full_width

    @pl.when(pl.program_id(0) == 0)
    def _():
        gain = sums[mp * dp_size, :, 2 * slots :]
        for other in range(1, dp_size):
            gain += sums[mp * dp_size + other, :, 2 * slots :]
        gain_out[...] = gain

    inverse = along_lanes(q_inverse[...], HD)
    unit = q_ref[0].astype(F32) * inverse
    scaled = q_part[...] * gain_q_ref[...]
    query_out[0] = ((scaled - unit * along_lanes(inner[:, :slots], HD)) * inverse).astype(LOW)
    inverse = along_lanes(notes[mine, :, :slots], HD)
    unit = k_ref[0].astype(F32) * inverse
    keep = jnp.where(lax.rem(mine, 2) == 0, 1.0, 0.0)
    total = own_part[...] + near_back[...].astype(F32) + side_back[...].astype(F32) * keep
    scaled = total[:slots] * gain_k_ref[...]
    key_out[0] = ((scaled - unit * along_lanes(inner[:, slots:], HD)) * inverse).astype(LOW)
    value_out[0] = total[slots:].astype(LOW)


def struct(shape, dtype=F32):
    return jax.ShapeDtypeStruct(shape, dtype)


def kernel_params():
    return pltpu.CompilerParams(vmem_limit_bytes=VMEM_LIMIT)


def on_device(q_proj, k_proj, values, grad_out, gain_q, gain_k, valid_count, segment):
    _, slots, local_width = q_proj.shape
    heads = local_width // HD
    mp_size, dp_size = lax.axis_size("mp"), lax.axis_size("dp")
    full_width = local_width * mp_size
    groups = lax.axis_size("tm")
    mine = lax.axis_index("tm")
    even = mine % 2 == 0
    tags = jnp.stack(
        [mine, valid_count[0, 0], segment[0, 0], lax.axis_index("mp"), lax.axis_index("dp")]
    ).astype(jnp.int32)
    gain_q = gain_q.reshape(1, local_width)
    gain_k = gain_k.reshape(1, local_width)
    smem = pl.BlockSpec(memory_space=pltpu.SMEM)

    two_on = [(i, i + 2) for i in range(groups - 2)]
    one_on = [(i, i + 1) for i in range(groups - 1)]
    pair = [(i, i ^ 1) for i in range(groups)]
    back = lambda moves: [(there, here) for here, there in moves]

    def head_blocks(first, rows):
        return pl.BlockSpec((rows, HD), lambda head: (0, first + head))

    def raw_blocks(first):
        return pl.BlockSpec((1, slots, HD), lambda head: (0, 0, first + head))

    def all_of(shape):
        return pl.BlockSpec(shape, lambda head: (0,) * len(shape))

    own, power = pl.pallas_call(
        prepare_kernel,
        grid=(heads,),
        in_specs=[raw_blocks(0)] * 3,
        out_specs=[head_blocks(0, 2 * slots), all_of((mp_size, 1, 2 * slots))],
        out_shape=[struct((2 * slots, local_width), LOW), struct((mp_size, 1, 2 * slots))],
        scratch_shapes=[pltpu.VMEM((2, slots, HD), F32)],
        compiler_params=kernel_params(),
        cost_estimate=pl.CostEstimate(flops=10**6, bytes_accessed=3 * 10**6, transcendentals=0),
    )(q_proj, k_proj, values)
    near = lax.ppermute(own, "tm", two_on)
    powers = lax.all_to_all(power, "mp", 0, 0, tiled=True)
    note, q_inverse = pl.pallas_call(
        functools.partial(roots_kernel, full_width),
        in_specs=[smem, pl.BlockSpec()],
        out_shape=[struct((groups, 1, slots + HD)), struct((1, slots))],
        compiler_params=kernel_params(),
    )(tags, powers)
    notes = lax.all_to_all(note, "tm", 0, 0, tiled=True)
    near, notes = lax.optimization_barrier((near, notes))
    side = lax.ppermute(jnp.where(even, own, near), "tm", one_on)
    swap = lax.ppermute(near, "tm", pair)

    state = jnp.zeros((8, 2 * local_width), F32)
    parts = []
    for first, last in CHUNKS:
        width = (last - first) * HD
        row_shape = (groups, 1, slots + 2 * local_width)
        q_part, own_part, near_part, side_part, swap_part, state, rows = pl.pallas_call(
            functools.partial(head_kernel, first, heads),
            grid=(last - first,),
            in_specs=[
                smem,
                all_of(notes.shape),
                all_of((1, slots)),
                head_blocks(first, 1),
                head_blocks(first, 1),
                raw_blocks(first),
                raw_blocks(first),
                *[head_blocks(first, 2 * slots)] * 4,
                all_of(state.shape),
            ],
            out_specs=[
                head_blocks(0, slots),
                *[head_blocks(0, 2 * slots)] * 4,
                all_of(state.shape),
                all_of(row_shape),
            ],
            out_shape=[
                struct((slots, width)),
                struct((2 * slots, width)),
                *[struct((2 * slots, width), LOW)] * 3,
                struct(state.shape),
                struct(row_shape),
            ],
            scratch_shapes=[
                pltpu.VMEM((4 * slots, slots), F32),
                pltpu.VMEM((4 * slots, slots), F32),
                pltpu.VMEM((4 * slots, slots), LOW),
                pltpu.VMEM((4 * slots, slots), LOW),
            ],
            compiler_params=kernel_params(),
            cost_estimate=pl.CostEstimate(
                flops=(last - first) * 40 * slots * slots * HD,
                bytes_accessed=(last - first) * 44 * slots * HD,
                transcendentals=(last - first) * 4 * slots * slots,
            ),
        )(tags, notes, q_inverse, gain_q, gain_k, q_proj, grad_out, own, near, side, swap, state)
        side_back = lax.ppermute(side_part, "tm", back(one_on))
        swap_back = lax.ppermute(swap_part, "tm", pair)
        near_sum = near_part.astype(F32) + swap_back.astype(F32)
        near_sum = near_sum + jnp.where(even, 0.0, side_back.astype(F32))
        near_sum = near_sum.astype(LOW)
        if last < heads:
            near_back = lax.ppermute(near_sum, "tm", back(two_on))
            early = near_sum
        else:
            rows, early = lax.optimization_barrier((rows, early))
            rows = lax.all_to_all(rows, "tm", 0, 0, tiled=True)
            rows, near_sum = lax.optimization_barrier((rows, near_sum))
            near_back = lax.ppermute(near_sum, "tm", back(two_on))
        parts.append((q_part, own_part, side_back, near_back))

    sums = pl.pallas_call(
        collect_kernel,
        out_shape=struct((mp_size * dp_size, 1, 2 * slots + 2 * local_width)),
        compiler_params=kernel_params(),
    )(state, rows)
    sums = lax.all_to_all(sums, ("mp", "dp"), 0, 0, tiled=True)

    outs = ()
    for (first, last), part in zip(CHUNKS, parts):
        specs = [
            smem,
            all_of(notes.shape),
            all_of((1, slots)),
            head_blocks(first, 1),
            head_blocks(first, 1),
            all_of(sums.shape),
            raw_blocks(first),
            raw_blocks(first),
            head_blocks(0, slots),
            *[head_blocks(0, 2 * slots)] * 3,
        ]
        *outs, gain = pl.pallas_call(
            functools.partial(finish_kernel, full_width, (mp_size, dp_size)),
            grid=(last - first,),
            in_specs=specs + [pl.BlockSpec(memory_space=pl.ANY)] * len(outs),
            out_specs=[*[raw_blocks(first)] * 3, all_of((1, 2 * local_width))],
            out_shape=[*[struct(q_proj.shape, LOW)] * 3, struct((1, 2 * local_width))],
            input_output_aliases={len(specs) + i: i for i in range(len(outs))},
            compiler_params=kernel_params(),
            cost_estimate=pl.CostEstimate(flops=10**6, bytes_accessed=5 * 10**6, transcendentals=0),
        )(tags, notes, q_inverse, gain_q, gain_k, sums, q_proj, k_proj, *part, *outs)
    return (*outs, gain[0, :local_width], gain[0, local_width:])


def solution(mesh):
    wide = P("dp", "tm", "mp")
    in_specs = (wide, wide, wide, wide, P("mp"), P("mp"), P("dp", "tm"), P("dp", "tm"))
    out_specs = (wide, wide, wide, P("mp"), P("mp"))
    return jax.shard_map(
        on_device, mesh=mesh, in_specs=in_specs, out_specs=out_specs, check_vma=False
    )
```

```python
import functools
import math

import jax
import jax.numpy as jnp
from jax import lax
from jax.experimental import pallas as pl
from jax.experimental.pallas import tpu as pltpu
from jax.sharding import PartitionSpec as P

HD = 128
EPSILON = 1e-06
MASKED = -1e30
STRIP = 48
F32, LOW = jnp.float32, jnp.bfloat16
VMEM_LIMIT = 60 * 1024 * 1024


def along_lanes(row, width):
    return jnp.transpose(jnp.broadcast_to(row, (width, row.shape[1])))


def row_sums(block):
    return jnp.sum(jnp.transpose(block), axis=0, keepdims=True)


def folded(block, op):
    return functools.reduce(op, [block[at : at + 8] for at in range(0, block.shape[0], 8)])


def power_kernel(q_ref, k_ref, power_out):
    slots, width = q_ref.shape[1:]
    for place, ref in enumerate((q_ref, k_ref)):
        total = jnp.zeros((slots, HD), F32)
        for at in range(0, width, HD):
            part = ref[0, :, at : at + HD].astype(F32)
            total += part * part
        row = row_sums(total)
        for device in range(power_out.shape[0]):
            power_out[device, :, place * slots : (place + 1) * slots] = row


def roots_kernel(full_width, tag_ref, power_ref, note_out, q_out):
    slots = q_out.shape[1]
    power = power_ref[0]
    for device in range(1, power_ref.shape[0]):
        power += power_ref[device]
    inverse = 1.0 / jnp.sqrt(power / full_width + EPSILON)
    q_out[...] = inverse[:, :slots]
    lane = lax.broadcasted_iota(jnp.int32, (1, HD), 1)
    valid = tag_ref[1].astype(F32)
    segment = tag_ref[2].astype(F32)
    tags = jnp.where(lane == 0, valid, jnp.where(lane == 1, segment, 0.0))
    for device in range(note_out.shape[0]):
        note_out[device, :, :slots] = inverse[:, slots:]
        note_out[device, :, slots:] = tags


def head_kernel(
    first, last, total_heads, skip, tag_ref, notes, q_inverse, gain_q_ref, gain_k_ref, q_ref, g_ref,
    own_ref, near_ref, side_ref, swap_ref, *rest,
):
    state_in = rest[0] if first else None
    q_out, own_out, near_out, side_out, swap_out, state_out, *rows_out = rest[skip:-6]
    score_ref, grad_ref, weight_low, grad_low, inverse_ref, inner_ref = rest[-6:]
    step = pl.program_id(0)
    slots = q_ref.shape[1]
    width = total_heads * HD
    scale = 1.0 / math.sqrt(HD)
    mine = tag_ref[0]
    even = lax.rem(mine, 2) == 0
    distances = (0, 2, jnp.where(even, 3, 1), jnp.where(even, 1, 3))
    gain_q = gain_q_ref[...]
    gain_k = gain_k_ref[...]
    segment = tag_ref[2].astype(F32)
    others = [jnp.maximum(mine - distance, 0) for distance in distances]

    @pl.when(step == 0)
    def _():
        for slot in range(4):
            inverse_ref[slot] = along_lanes(notes[others[slot], :, :slots], HD)
        inverse_ref[4] = along_lanes(q_inverse[...], HD)
        inner_ref[...] = jnp.zeros_like(inner_ref)
        if first:
            state_out[...] = state_in[...]
        else:
            state_out[...] = jnp.zeros_like(state_out)

    q_unit = q_ref[0].astype(F32) * inverse_ref[4]
    q_norm = (q_unit * gain_q).astype(LOW)
    live = lax.broadcasted_iota(jnp.int32, (slots, HD), 0) < tag_ref[1]
    g_live = jnp.where(live, g_ref[0].astype(F32), 0.0).astype(LOW)
    q_side = jnp.transpose(q_norm)
    g_side = jnp.transpose(g_live)
    lanes = lax.broadcasted_iota(jnp.int32, (STRIP, slots), 0).astype(F32)
    refs = (own_ref, near_ref, side_ref, swap_ref)
    k_norms, limits = [], []
    for slot, ref in enumerate(refs):
        tags = notes[others[slot], :, slots:]
        same = (tags[:, 1:2] == segment) & (mine >= distances[slot])
        limits.append(jnp.where(same, tags[:, 0:1], 0.0))
        k_norm = (ref[:slots, :].astype(F32) * inverse_ref[slot] * gain_k).astype(LOW)
        k_norms.append(k_norm)
        rows = slice(slot * slots, (slot + 1) * slots)
        score_ref[rows, :] = jnp.dot(k_norm, q_side, preferred_element_type=F32)
        grad_ref[rows, :] = jnp.dot(ref[slots:, :], g_side, preferred_element_type=F32)
    strips = [(slot, at) for slot in range(4) for at in range(0, slots, STRIP)]
    top = jnp.full((8, slots), MASKED, F32)
    for slot, at in strips:
        base = slot * slots + at
        included = lanes < limits[slot] - at
        score = jnp.where(included, score_ref[base : base + STRIP, :], MASKED)
        top = jnp.maximum(top, folded(score, jnp.maximum))
    top = jnp.max(top, axis=0, keepdims=True)
    total = jnp.zeros((8, slots), F32)
    delta = jnp.zeros((8, slots), F32)
    for slot, at in strips:
        base = slot * slots + at
        included = lanes < limits[slot] - at
        score = jnp.where(included, score_ref[base : base + STRIP, :], MASKED)
        exponent = jnp.exp((score - top) * scale)
        score_ref[base : base + STRIP, :] = exponent
        total += folded(exponent, jnp.add)
        delta += folded(exponent * grad_ref[base : base + STRIP, :], jnp.add)
    inverse_sum = 1.0 / jnp.sum(total, axis=0, keepdims=True)
    delta = jnp.sum(delta, axis=0, keepdims=True) * inverse_sum
    q_turned = jnp.zeros((HD, slots), F32)
    k_gain = jnp.zeros((1, HD), F32)
    for slot, out in enumerate((own_out, near_out, side_out, swap_out)):
        for at in range(0, slots, STRIP):
            rows = slice(slot * slots + at, slot * slots + at + STRIP)
            weight = score_ref[rows, :] * inverse_sum
            weight_low[rows, :] = weight.astype(LOW)
            grad_low[rows, :] = (weight * (grad_ref[rows, :] - delta)).astype(LOW)
        rows = slice(slot * slots, (slot + 1) * slots)
        q_turned += jnp.dot(
            jnp.transpose(k_norms[slot]), grad_low[rows, :], preferred_element_type=F32
        )
        k_part = jnp.dot(grad_low[rows, :], q_norm, preferred_element_type=F32) * scale
        v_part = jnp.dot(weight_low[rows, :], g_live, preferred_element_type=F32)
        out[:slots, :] = k_part.astype(out.dtype)
        out[slots:, :] = v_part.astype(out.dtype)
        product = k_part * (refs[slot][:slots, :].astype(F32) * inverse_ref[slot])
        k_gain += jnp.sum(product, axis=0, keepdims=True)
        inner_ref[slot] += product * gain_k
    q_part = jnp.transpose(q_turned) * scale
    q_out[...] = q_part
    product = q_part * q_unit
    inner_ref[4] += product * gain_q
    at = (first + step) * HD
    state_out[5:6, pl.ds(pl.multiple_of(at, HD), HD)] = jnp.sum(product, axis=0, keepdims=True)
    state_out[5:6, pl.ds(pl.multiple_of(width + at, HD), HD)] = k_gain

    @pl.when(step == last - first - 1)
    def _():
        for slot in range(5):
            state_out[slot : slot + 1, :slots] += row_sums(inner_ref[slot])
        if last == total_heads:
            (rows_ref,) = rows_out
            for device in range(rows_ref.shape[0]):
                rows_ref[device, :, :slots] = jnp.zeros((1, slots), F32)
                rows_ref[device, :, slots:] = state_out[5:6, :]
            for slot, distance in enumerate(distances):
                @pl.when(mine >= distance)
                def _():
                    rows_ref[mine - distance, :, :slots] = state_out[slot : slot + 1, :slots]


def head_blocks(first, rows):
    return pl.BlockSpec((rows, HD), lambda head: (0, first + head))


def raw_blocks(first, slots):
    return pl.BlockSpec((1, slots, HD), lambda head: (0, 0, first + head))


def all_of(shape):
    return pl.BlockSpec(shape, lambda *_: (0,) * len(shape))


def attend(
    first, last, chunk, heads, groups, tags, notes, q_inverse, gain_q, gain_k, q, g, halo, state, outs
):
    slots = q.shape[1]
    width = (chunk[1] - chunk[0]) * HD
    place = first - chunk[0]
    state_shape = (8, 2 * heads * HD)
    row_shape = (groups, 1, slots + 2 * heads * HD)
    final = last == heads
    known = 11 + len(state)
    return pl.pallas_call(
        functools.partial(head_kernel, first, last, heads, len(state) + len(outs)),
        grid=(last - first,),
        in_specs=[
            pl.BlockSpec(memory_space=pltpu.SMEM),
            all_of(notes.shape),
            all_of((1, slots)),
            head_blocks(first, 1),
            head_blocks(first, 1),
            raw_blocks(first, slots),
            raw_blocks(first, slots),
            *[head_blocks(first, 2 * slots)] * 4,
            *[all_of(state_shape)] * len(state),
            *[pl.BlockSpec(memory_space=pl.ANY)] * len(outs),
        ],
        out_specs=[
            head_blocks(place, slots),
            *[head_blocks(place, 2 * slots)] * 4,
            all_of(state_shape),
            *[all_of(row_shape)] * final,
        ],
        out_shape=[
            struct((slots, width)),
            struct((2 * slots, width)),
            *[struct((2 * slots, width), LOW)] * 3,
            struct(state_shape),
            *[struct(row_shape)] * final,
        ],
        scratch_shapes=[
            pltpu.VMEM((4 * slots, slots), F32),
            pltpu.VMEM((4 * slots, slots), F32),
            pltpu.VMEM((4 * slots, slots), LOW),
            pltpu.VMEM((4 * slots, slots), LOW),
            pltpu.VMEM((5, slots, HD), F32),
            pltpu.VMEM((5, slots, HD), F32),
        ],
        input_output_aliases={known + i: i for i in range(len(outs))},
        compiler_params=kernel_params(),
        cost_estimate=pl.CostEstimate(
            flops=(last - first) * 40 * slots * slots * HD,
            bytes_accessed=(last - first) * 44 * slots * HD,
            transcendentals=(last - first) * 4 * slots * slots,
        ),
    )(tags, notes, q_inverse, gain_q, gain_k, q, g, *halo, *state, *outs)


def collect_kernel(state_ref, rows_ref, inner_out, gain_out):
    slots = inner_out.shape[2] // 2
    total = rows_ref[0]
    for device in range(1, rows_ref.shape[0]):
        total += rows_ref[device]
    for device in range(inner_out.shape[0]):
        inner_out[device, :, :slots] = state_ref[4:5, :slots]
        inner_out[device, :, slots:] = total[:, :slots]
    for device in range(gain_out.shape[0]):
        gain_out[device] = total[:, slots:]


def total_of(sums):
    total = sums[0]
    for other in range(1, sums.shape[0]):
        total += sums[other]
    return total


def query_kernel(
    full_width, q_inverse, gain_ref, inners, q_ref, q_part, query_out, turned
):
    rows, width = q_ref.shape[1:]
    slots = q_inverse.shape[1]
    step = pl.program_id(0)

    @pl.when(step == 0)
    def _():
        inner = total_of(inners)[:, :slots] / full_width
        turned[0] = along_lanes(q_inverse[...], HD)
        turned[1] = along_lanes(inner, HD) * turned[0]

    here = pl.ds(pl.multiple_of(step * rows, 16), rows)
    inverse, inner = turned[0, here, :], turned[1, here, :]
    for at in range(0, width, HD):
        lanes = slice(at, at + HD)
        scaled = q_part[:, lanes] * gain_ref[:, lanes]
        query_out[0, :, lanes] = ((scaled - q_ref[0, :, lanes].astype(F32) * inner) * inverse).astype(LOW)


def key_kernel(
    full_width, tag_ref, notes, gain_ref, inners, k_ref, k_own, v_own, k_side, v_side, k_near,
    v_near, key_out, value_out, turned,
):
    rows, width = k_ref.shape[1:]
    slots = turned.shape[1]
    mine = tag_ref[0]
    step = pl.program_id(0)

    @pl.when(step == 0)
    def _():
        inner = total_of(inners)[:, slots:] / full_width
        turned[0] = along_lanes(notes[mine, :, :slots], HD)
        turned[1] = along_lanes(inner, HD) * turned[0]

    here = pl.ds(pl.multiple_of(step * rows, 16), rows)
    inverse, inner = turned[0, here, :], turned[1, here, :]
    keep = jnp.where(lax.rem(mine, 2) == 0, 1.0, 0.0)
    for at in range(0, width, HD):
        lanes = slice(at, at + HD)
        total = k_own[:, lanes] + k_near[:, lanes].astype(F32)
        total += k_side[:, lanes].astype(F32) * keep
        scaled = total * gain_ref[:, lanes]
        key_out[0, :, lanes] = ((scaled - k_ref[0, :, lanes].astype(F32) * inner) * inverse).astype(LOW)
        total = v_own[:, lanes] + v_near[:, lanes].astype(F32)
        value_out[0, :, lanes] = (total + v_side[:, lanes].astype(F32) * keep).astype(LOW)


def struct(shape, dtype=F32):
    return jax.ShapeDtypeStruct(shape, dtype)


def kernel_params(limit=VMEM_LIMIT):
    return pltpu.CompilerParams(vmem_limit_bytes=limit)


def on_device(q_proj, k_proj, values, grad_out, gain_q, gain_k, valid_count, segment):
    _, slots, local_width = q_proj.shape
    heads = local_width // HD
    mp_size, dp_size = lax.axis_size("mp"), lax.axis_size("dp")
    full_width = local_width * mp_size
    groups = lax.axis_size("tm")
    mine = lax.axis_index("tm")
    even = mine % 2 == 0
    tags = jnp.stack([mine, valid_count[0, 0], segment[0, 0]]).astype(jnp.int32)
    gain_q = gain_q.reshape(1, local_width)
    gain_k = gain_k.reshape(1, local_width)
    smem = pl.BlockSpec(memory_space=pltpu.SMEM)

    two_on = [(i, i + 2) for i in range(groups - 2)]
    one_on = [(i, i + 1) for i in range(groups - 1)]
    pair = [(i, i ^ 1) for i in range(groups)]
    back = lambda moves: [(there, here) for here, there in moves]

    anywhere = pl.BlockSpec(memory_space=pl.ANY)
    own = jnp.concatenate([k_proj[0], values[0]], axis=0)
    near = lax.ppermute(own, "tm", two_on)
    power = pl.pallas_call(
        power_kernel,
        out_shape=struct((mp_size, 1, 2 * slots)),
        compiler_params=kernel_params(),
        cost_estimate=pl.CostEstimate(flops=10**6, bytes_accessed=10**6, transcendentals=0),
    )(q_proj, k_proj)
    powers = lax.all_to_all(power, "mp", 0, 0, tiled=True)
    note, q_inverse = pl.pallas_call(
        functools.partial(roots_kernel, full_width),
        in_specs=[smem, pl.BlockSpec()],
        out_shape=[struct((groups, 1, slots + HD)), struct((1, slots))],
        compiler_params=kernel_params(),
    )(tags, powers)
    near, note = lax.optimization_barrier((near, note))
    passed, note = lax.optimization_barrier((jnp.where(even, own, near), note))
    side = lax.ppermute(passed, "tm", one_on)
    swap = lax.ppermute(near, "tm", pair)
    notes = lax.all_to_all(note, "tm", 0, 0, tiled=True)

    q_part, own_part, near_part, side_part, swap_part, state, rows = attend(
        0, heads, (0, heads), heads, groups, tags, notes, q_inverse, gain_q, gain_k, q_proj,
        grad_out, (own, near, side, swap), [], [],
    )
    side_back = lax.ppermute(side_part, "tm", back(one_on))
    swap_back = lax.ppermute(swap_part, "tm", pair)
    rows = lax.all_to_all(rows, "tm", 0, 0, tiled=True)
    inners, gains = pl.pallas_call(
        collect_kernel,
        out_shape=[struct((mp_size, 1, 2 * slots)), struct((dp_size, 1, 2 * local_width))],
        compiler_params=kernel_params(),
    )(state, rows)
    near_sum = near_part.astype(F32) + swap_back.astype(F32)
    near_sum = (near_sum + jnp.where(even, 0.0, side_back.astype(F32))).astype(LOW)
    inners, near_sum = lax.optimization_barrier((inners, near_sum))
    near_back = lax.ppermute(near_sum, "tm", back(two_on))
    inners = lax.all_to_all(inners, "mp", 0, 0, tiled=True)
    gains, inners = lax.optimization_barrier((gains, inners))
    gains = lax.all_to_all(gains, "dp", 0, 0, tiled=True)

    steps = 4
    block = slots // steps
    raw = pl.BlockSpec((1, block, local_width), lambda step: (0, step, 0))
    upper = pl.BlockSpec((block, local_width), lambda step: (step, 0))
    lower = pl.BlockSpec((block, local_width), lambda step: (step + steps, 0))
    query_grad = pl.pallas_call(
        functools.partial(query_kernel, full_width),
        grid=(steps,),
        in_specs=[
            all_of((1, slots)),
            all_of((1, local_width)),
            all_of(inners.shape),
            raw,
            upper,
        ],
        out_specs=raw,
        out_shape=struct(q_proj.shape, LOW),
        scratch_shapes=[pltpu.VMEM((2, slots, HD), F32)],
        compiler_params=kernel_params(16 * 1024 * 1024),
        cost_estimate=pl.CostEstimate(flops=10**6, bytes_accessed=3 * 10**6, transcendentals=0),
    )(q_inverse, gain_q, inners, q_proj, q_part)
    key_grad, value_grad = pl.pallas_call(
        functools.partial(key_kernel, full_width),
        grid=(steps,),
        in_specs=[
            smem,
            all_of(notes.shape),
            all_of((1, local_width)),
            all_of(inners.shape),
            raw,
            *[upper, lower] * 3,
        ],
        out_specs=[raw] * 2,
        out_shape=[struct(q_proj.shape, LOW)] * 2,
        scratch_shapes=[pltpu.VMEM((2, slots, HD), F32)],
        compiler_params=kernel_params(16 * 1024 * 1024),
        cost_estimate=pl.CostEstimate(flops=10**6, bytes_accessed=5 * 10**6, transcendentals=0),
    )(
        tags, notes, gain_k, inners, k_proj,
        own_part, own_part, side_back, side_back, near_back, near_back,
    )
    gain_sum = jnp.sum(gains[:, 0], axis=0)
    return query_grad, key_grad, value_grad, gain_sum[:local_width], gain_sum[local_width:]


def solution(mesh):
    wide = P("dp", "tm", "mp")
    in_specs = (wide, wide, wide, wide, P("mp"), P("mp"), P("dp", "tm"), P("dp", "tm"))
    out_specs = (wide, wide, wide, P("mp"), P("mp"))
    return jax.shard_map(
        on_device, mesh=mesh, in_specs=in_specs, out_specs=out_specs, check_vma=False
    )
```

```python
import functools
import math

import jax
import jax.numpy as jnp
from jax import lax
from jax.experimental import pallas as pl
from jax.experimental.pallas import tpu as pltpu
from jax.sharding import PartitionSpec as P

HD = 128
EPSILON = 1e-06
MASKED = -1e30
STRIP = 48
F32, LOW = jnp.float32, jnp.bfloat16
VMEM_LIMIT = 60 * 1024 * 1024


def along_lanes(row, width):
    return jnp.transpose(jnp.broadcast_to(row, (width, row.shape[1])))


def row_sums(block):
    return jnp.sum(jnp.transpose(block), axis=0, keepdims=True)


def folded(block, op):
    return functools.reduce(op, [block[at : at + 8] for at in range(0, block.shape[0], 8)])


def power_kernel(q_ref, k_ref, power_out):
    slots, width = q_ref.shape[1:]
    for place, ref in enumerate((q_ref, k_ref)):
        total = jnp.zeros((slots, HD), F32)
        for at in range(0, width, HD):
            part = ref[0, :, at : at + HD].astype(F32)
            total += part * part
        row = row_sums(total)
        for device in range(power_out.shape[0]):
            power_out[device, :, place * slots : (place + 1) * slots] = row


def roots_kernel(full_width, tag_ref, power_ref, note_out, q_out):
    slots = q_out.shape[1]
    power = power_ref[0]
    for device in range(1, power_ref.shape[0]):
        power += power_ref[device]
    inverse = 1.0 / jnp.sqrt(power / full_width + EPSILON)
    q_out[...] = inverse[:, :slots]
    lane = lax.broadcasted_iota(jnp.int32, (1, HD), 1)
    valid = tag_ref[1].astype(F32)
    segment = tag_ref[2].astype(F32)
    tags = jnp.where(lane == 0, valid, jnp.where(lane == 1, segment, 0.0))
    for device in range(note_out.shape[0]):
        note_out[device, :, :slots] = inverse[:, slots:]
        note_out[device, :, slots:] = tags


def head_kernel(
    first, last, total_heads, skip, tag_ref, notes, q_inverse, gain_q_ref, gain_k_ref, q_ref, g_ref,
    own_ref, near_ref, side_ref, swap_ref, *rest,
):
    state_in = rest[0] if first else None
    q_out, own_out, near_out, side_out, swap_out, state_out, *rows_out = rest[skip:-6]
    score_ref, grad_ref, weight_low, grad_low, inverse_ref, inner_ref = rest[-6:]
    step = pl.program_id(0)
    slots = q_ref.shape[1]
    width = total_heads * HD
    scale = 1.0 / math.sqrt(HD)
    steep = scale / math.log(2.0)
    mine = tag_ref[0]
    even = lax.rem(mine, 2) == 0
    distances = (0, 2, jnp.where(even, 3, 1), jnp.where(even, 1, 3))
    gain_q = gain_q_ref[...]
    gain_k = gain_k_ref[...]
    segment = tag_ref[2].astype(F32)
    others = [jnp.maximum(mine - distance, 0) for distance in distances]

    @pl.when(step == 0)
    def _():
        for slot in range(4):
            inverse_ref[slot] = along_lanes(notes[others[slot], :, :slots], HD)
        inverse_ref[4] = along_lanes(q_inverse[...], HD)
        inner_ref[...] = jnp.zeros_like(inner_ref)
        if first:
            state_out[...] = state_in[...]
        else:
            state_out[...] = jnp.zeros_like(state_out)

    q_unit = q_ref[0].astype(F32) * inverse_ref[4]
    q_norm = (q_unit * gain_q).astype(LOW)
    live = lax.broadcasted_iota(jnp.int32, (slots, HD), 0) < tag_ref[1]
    g_live = jnp.where(live, g_ref[0].astype(F32), 0.0).astype(LOW)
    q_side = jnp.transpose(q_norm)
    g_side = jnp.transpose(g_live)
    lanes = lax.broadcasted_iota(jnp.int32, (STRIP, slots), 0).astype(F32)
    refs = (own_ref, near_ref, side_ref, swap_ref)
    k_norms, limits = [], []
    for slot, ref in enumerate(refs):
        tags = notes[others[slot], :, slots:]
        same = (tags[:, 1:2] == segment) & (mine >= distances[slot])
        limits.append(jnp.where(same, tags[:, 0:1], 0.0))
        k_norm = (ref[:slots, :].astype(F32) * inverse_ref[slot] * gain_k).astype(LOW)
        k_norms.append(k_norm)
        rows = slice(slot * slots, (slot + 1) * slots)
        score_ref[rows, :] = jnp.dot(k_norm, q_side, preferred_element_type=F32)
        grad_ref[rows, :] = jnp.dot(ref[slots:, :], g_side, preferred_element_type=F32)
    strips = [(slot, at) for slot in range(4) for at in range(0, slots, STRIP)]
    top = jnp.full((8, slots), MASKED, F32)
    for slot, at in strips:
        base = slot * slots + at
        included = lanes < limits[slot] - at
        score = jnp.where(included, score_ref[base : base + STRIP, :], MASKED)
        top = jnp.maximum(top, folded(score, jnp.maximum))
    top = jnp.max(top, axis=0, keepdims=True)
    total = jnp.zeros((8, slots), F32)
    delta = jnp.zeros((8, slots), F32)
    for slot, at in strips:
        base = slot * slots + at
        included = lanes < limits[slot] - at
        score = jnp.where(included, score_ref[base : base + STRIP, :], MASKED)
        exponent = jnp.exp2((score - top) * steep)
        score_ref[base : base + STRIP, :] = exponent
        total += folded(exponent, jnp.add)
        delta += folded(exponent * grad_ref[base : base + STRIP, :], jnp.add)
    inverse_sum = 1.0 / jnp.sum(total, axis=0, keepdims=True)
    delta = jnp.sum(delta, axis=0, keepdims=True) * inverse_sum
    q_turned = jnp.zeros((HD, slots), F32)
    k_gain = jnp.zeros((1, HD), F32)
    for slot, out in enumerate((own_out, near_out, side_out, swap_out)):
        for at in range(0, slots, STRIP):
            rows = slice(slot * slots + at, slot * slots + at + STRIP)
            weight = score_ref[rows, :] * inverse_sum
            weight_low[rows, :] = weight.astype(LOW)
            grad_low[rows, :] = (weight * (grad_ref[rows, :] - delta)).astype(LOW)
        rows = slice(slot * slots, (slot + 1) * slots)
        q_turned += jnp.dot(
            jnp.transpose(k_norms[slot]), grad_low[rows, :], preferred_element_type=F32
        )
        k_part = jnp.dot(grad_low[rows, :], q_norm, preferred_element_type=F32) * scale
        v_part = jnp.dot(weight_low[rows, :], g_live, preferred_element_type=F32)
        out[:slots, :] = k_part.astype(out.dtype)
        out[slots:, :] = v_part.astype(out.dtype)
        product = k_part * (refs[slot][:slots, :].astype(F32) * inverse_ref[slot])
        k_gain += jnp.sum(product, axis=0, keepdims=True)
        inner_ref[slot] += product * gain_k
    q_part = jnp.transpose(q_turned) * scale
    q_out[...] = q_part
    product = q_part * q_unit
    inner_ref[4] += product * gain_q
    at = (first + step) * HD
    state_out[5:6, pl.ds(pl.multiple_of(at, HD), HD)] = jnp.sum(product, axis=0, keepdims=True)
    state_out[5:6, pl.ds(pl.multiple_of(width + at, HD), HD)] = k_gain

    @pl.when(step == last - first - 1)
    def _():
        for slot in range(5):
            state_out[slot : slot + 1, :slots] += row_sums(inner_ref[slot])
        if last == total_heads:
            (rows_ref,) = rows_out
            for device in range(rows_ref.shape[0]):
                rows_ref[device, :, :slots] = jnp.zeros((1, slots), F32)
                rows_ref[device, :, slots:] = state_out[5:6, :]
            for slot, distance in enumerate(distances):
                @pl.when(mine >= distance)
                def _():
                    rows_ref[mine - distance, :, :slots] = state_out[slot : slot + 1, :slots]


def head_blocks(first, rows):
    return pl.BlockSpec((rows, HD), lambda head: (0, first + head))


def raw_blocks(first, slots):
    return pl.BlockSpec((1, slots, HD), lambda head: (0, 0, first + head))


def all_of(shape):
    return pl.BlockSpec(shape, lambda *_: (0,) * len(shape))


def attend(
    first, last, chunk, heads, groups, tags, notes, q_inverse, gain_q, gain_k, q, g, halo, state, outs
):
    slots = q.shape[1]
    width = (chunk[1] - chunk[0]) * HD
    place = first - chunk[0]
    state_shape = (8, 2 * heads * HD)
    row_shape = (groups, 1, slots + 2 * heads * HD)
    final = last == heads
    known = 11 + len(state)
    return pl.pallas_call(
        functools.partial(head_kernel, first, last, heads, len(state) + len(outs)),
        grid=(last - first,),
        in_specs=[
            pl.BlockSpec(memory_space=pltpu.SMEM),
            all_of(notes.shape),
            all_of((1, slots)),
            head_blocks(first, 1),
            head_blocks(first, 1),
            raw_blocks(first, slots),
            raw_blocks(first, slots),
            *[head_blocks(first, 2 * slots)] * 4,
            *[all_of(state_shape)] * len(state),
            *[pl.BlockSpec(memory_space=pl.ANY)] * len(outs),
        ],
        out_specs=[
            head_blocks(place, slots),
            *[head_blocks(place, 2 * slots)] * 4,
            all_of(state_shape),
            *[all_of(row_shape)] * final,
        ],
        out_shape=[
            struct((slots, width)),
            struct((2 * slots, width)),
            *[struct((2 * slots, width), LOW)] * 3,
            struct(state_shape),
            *[struct(row_shape)] * final,
        ],
        scratch_shapes=[
            pltpu.VMEM((4 * slots, slots), F32),
            pltpu.VMEM((4 * slots, slots), F32),
            pltpu.VMEM((4 * slots, slots), LOW),
            pltpu.VMEM((4 * slots, slots), LOW),
            pltpu.VMEM((5, slots, HD), F32),
            pltpu.VMEM((5, slots, HD), F32),
        ],
        input_output_aliases={known + i: i for i in range(len(outs))},
        compiler_params=kernel_params(),
        cost_estimate=pl.CostEstimate(
            flops=(last - first) * 40 * slots * slots * HD,
            bytes_accessed=(last - first) * 44 * slots * HD,
            transcendentals=(last - first) * 4 * slots * slots,
        ),
    )(tags, notes, q_inverse, gain_q, gain_k, q, g, *halo, *state, *outs)


def collect_kernel(state_ref, rows_ref, inner_out, gain_out):
    slots = inner_out.shape[2] // 2
    total = rows_ref[0]
    for device in range(1, rows_ref.shape[0]):
        total += rows_ref[device]
    for device in range(inner_out.shape[0]):
        inner_out[device, :, :slots] = state_ref[4:5, :slots]
        inner_out[device, :, slots:] = total[:, :slots]
    for device in range(gain_out.shape[0]):
        gain_out[device] = total[:, slots:]


def total_of(sums):
    total = sums[0]
    for other in range(1, sums.shape[0]):
        total += sums[other]
    return total


def query_kernel(
    full_width, q_inverse, gain_ref, inners, q_ref, q_part, query_out, turned
):
    rows, width = q_ref.shape[1:]
    slots = q_inverse.shape[1]
    step = pl.program_id(0)

    @pl.when(step == 0)
    def _():
        inner = total_of(inners)[:, :slots] / full_width
        turned[0] = along_lanes(q_inverse[...], HD)
        turned[1] = along_lanes(inner, HD) * turned[0]

    here = pl.ds(pl.multiple_of(step * rows, 16), rows)
    inverse, inner = turned[0, here, :], turned[1, here, :]
    for at in range(0, width, HD):
        lanes = slice(at, at + HD)
        scaled = q_part[:, lanes] * gain_ref[:, lanes]
        query_out[0, :, lanes] = ((scaled - q_ref[0, :, lanes].astype(F32) * inner) * inverse).astype(LOW)


def key_kernel(
    full_width, tag_ref, notes, gain_ref, inners, k_ref, k_own, v_own, k_side, v_side, k_near,
    v_near, key_out, value_out, turned,
):
    rows, width = k_ref.shape[1:]
    slots = turned.shape[1]
    mine = tag_ref[0]
    step = pl.program_id(0)

    @pl.when(step == 0)
    def _():
        inner = total_of(inners)[:, slots:] / full_width
        turned[0] = along_lanes(notes[mine, :, :slots], HD)
        turned[1] = along_lanes(inner, HD) * turned[0]

    here = pl.ds(pl.multiple_of(step * rows, 16), rows)
    inverse, inner = turned[0, here, :], turned[1, here, :]
    keep = jnp.where(lax.rem(mine, 2) == 0, 1.0, 0.0)
    for at in range(0, width, HD):
        lanes = slice(at, at + HD)
        total = k_own[:, lanes] + k_near[:, lanes].astype(F32)
        total += k_side[:, lanes].astype(F32) * keep
        scaled = total * gain_ref[:, lanes]
        key_out[0, :, lanes] = ((scaled - k_ref[0, :, lanes].astype(F32) * inner) * inverse).astype(LOW)
        total = v_own[:, lanes] + v_near[:, lanes].astype(F32)
        value_out[0, :, lanes] = (total + v_side[:, lanes].astype(F32) * keep).astype(LOW)


def struct(shape, dtype=F32):
    return jax.ShapeDtypeStruct(shape, dtype)


def kernel_params(limit=VMEM_LIMIT):
    return pltpu.CompilerParams(vmem_limit_bytes=limit)


def on_device(q_proj, k_proj, values, grad_out, gain_q, gain_k, valid_count, segment):
    _, slots, local_width = q_proj.shape
    heads = local_width // HD
    mp_size, dp_size = lax.axis_size("mp"), lax.axis_size("dp")
    full_width = local_width * mp_size
    groups = lax.axis_size("tm")
    mine = lax.axis_index("tm")
    even = mine % 2 == 0
    tags = jnp.stack([mine, valid_count[0, 0], segment[0, 0]]).astype(jnp.int32)
    gain_q = gain_q.reshape(1, local_width)
    gain_k = gain_k.reshape(1, local_width)
    smem = pl.BlockSpec(memory_space=pltpu.SMEM)

    two_on = [(i, i + 2) for i in range(groups - 2)]
    one_on = [(i, i + 1) for i in range(groups - 1)]
    pair = [(i, i ^ 1) for i in range(groups)]
    back = lambda moves: [(there, here) for here, there in moves]

    anywhere = pl.BlockSpec(memory_space=pl.ANY)
    own = jnp.concatenate([k_proj[0], values[0]], axis=0)
    near = lax.ppermute(own, "tm", two_on)
    power = pl.pallas_call(
        power_kernel,
        out_shape=struct((mp_size, 1, 2 * slots)),
        compiler_params=kernel_params(),
        cost_estimate=pl.CostEstimate(flops=10**6, bytes_accessed=10**6, transcendentals=0),
    )(q_proj, k_proj)
    powers = lax.all_to_all(power, "mp", 0, 0, tiled=True)
    note, q_inverse = pl.pallas_call(
        functools.partial(roots_kernel, full_width),
        in_specs=[smem, pl.BlockSpec()],
        out_shape=[struct((groups, 1, slots + HD)), struct((1, slots))],
        compiler_params=kernel_params(),
    )(tags, powers)
    near, note = lax.optimization_barrier((near, note))
    passed, note = lax.optimization_barrier((jnp.where(even, own, near), note))
    side = lax.ppermute(passed, "tm", one_on)
    swap = lax.ppermute(near, "tm", pair)
    notes = lax.all_to_all(note, "tm", 0, 0, tiled=True)

    q_part, own_part, near_part, side_part, swap_part, state, rows = attend(
        0, heads, (0, heads), heads, groups, tags, notes, q_inverse, gain_q, gain_k, q_proj,
        grad_out, (own, near, side, swap), [], [],
    )
    side_back = lax.ppermute(side_part, "tm", back(one_on))
    swap_back = lax.ppermute(swap_part, "tm", pair)
    rows = lax.all_to_all(rows, "tm", 0, 0, tiled=True)
    inners, gains = pl.pallas_call(
        collect_kernel,
        out_shape=[struct((mp_size, 1, 2 * slots)), struct((dp_size, 1, 2 * local_width))],
        compiler_params=kernel_params(),
    )(state, rows)
    near_sum = near_part.astype(F32) + swap_back.astype(F32)
    near_sum = (near_sum + jnp.where(even, 0.0, side_back.astype(F32))).astype(LOW)
    inners, near_sum = lax.optimization_barrier((inners, near_sum))
    near_back = lax.ppermute(near_sum, "tm", back(two_on))
    inners = lax.all_to_all(inners, "mp", 0, 0, tiled=True)
    gains, inners = lax.optimization_barrier((gains, inners))
    gains = lax.all_to_all(gains, "dp", 0, 0, tiled=True)

    steps = 4
    block = slots // steps
    raw = pl.BlockSpec((1, block, local_width), lambda step: (0, step, 0))
    upper = pl.BlockSpec((block, local_width), lambda step: (step, 0))
    lower = pl.BlockSpec((block, local_width), lambda step: (step + steps, 0))
    query_grad = pl.pallas_call(
        functools.partial(query_kernel, full_width),
        grid=(steps,),
        in_specs=[
            all_of((1, slots)),
            all_of((1, local_width)),
            all_of(inners.shape),
            raw,
            upper,
        ],
        out_specs=raw,
        out_shape=struct(q_proj.shape, LOW),
        scratch_shapes=[pltpu.VMEM((2, slots, HD), F32)],
        compiler_params=kernel_params(16 * 1024 * 1024),
        cost_estimate=pl.CostEstimate(flops=10**6, bytes_accessed=3 * 10**6, transcendentals=0),
    )(q_inverse, gain_q, inners, q_proj, q_part)
    key_grad, value_grad = pl.pallas_call(
        functools.partial(key_kernel, full_width),
        grid=(steps,),
        in_specs=[
            smem,
            all_of(notes.shape),
            all_of((1, local_width)),
            all_of(inners.shape),
            raw,
            *[upper, lower] * 3,
        ],
        out_specs=[raw] * 2,
        out_shape=[struct(q_proj.shape, LOW)] * 2,
        scratch_shapes=[pltpu.VMEM((2, slots, HD), F32)],
        compiler_params=kernel_params(16 * 1024 * 1024),
        cost_estimate=pl.CostEstimate(flops=10**6, bytes_accessed=5 * 10**6, transcendentals=0),
    )(
        tags, notes, gain_k, inners, k_proj,
        own_part, own_part, side_back, side_back, near_back, near_back,
    )
    gains, key_grad = lax.optimization_barrier((gains, key_grad))
    gain_sum = jnp.sum(gains[:, 0], axis=0)
    return query_grad, key_grad, value_grad, gain_sum[:local_width], gain_sum[local_width:]


def solution(mesh):
    wide = P("dp", "tm", "mp")
    in_specs = (wide, wide, wide, wide, P("mp"), P("mp"), P("dp", "tm"), P("dp", "tm"))
    out_specs = (wide, wide, wide, P("mp"), P("mp"))
    return jax.shard_map(
        on_device, mesh=mesh, in_specs=in_specs, out_specs=out_specs, check_vma=False
    )
```

```python
import functools
import math

import jax
import jax.numpy as jnp
from jax import lax
from jax.experimental import pallas as pl
from jax.experimental.pallas import tpu as pltpu
from jax.sharding import PartitionSpec as P

HD = 128
EPSILON = 1e-06
MASKED = -1e30
STRIP = 48
F32, LOW = jnp.float32, jnp.bfloat16
VMEM_LIMIT = 60 * 1024 * 1024


def along_lanes(row, width):
    return jnp.transpose(jnp.broadcast_to(row, (width, row.shape[1])))


def row_sums(block):
    return jnp.sum(jnp.transpose(block), axis=0, keepdims=True)


def folded(block, op):
    return functools.reduce(op, [block[at : at + 8] for at in range(0, block.shape[0], 8)])


def power_kernel(q_ref, k_ref, power_out):
    slots, width = q_ref.shape[1:]
    for place, ref in enumerate((q_ref, k_ref)):
        total = jnp.zeros((slots, HD), F32)
        for at in range(0, width, HD):
            part = ref[0, :, at : at + HD].astype(F32)
            total += part * part
        row = row_sums(total)
        for device in range(power_out.shape[0]):
            power_out[device, :, place * slots : (place + 1) * slots] = row


def roots_kernel(full_width, tag_ref, power_ref, note_out, q_out):
    slots = q_out.shape[1]
    power = power_ref[0]
    for device in range(1, power_ref.shape[0]):
        power += power_ref[device]
    inverse = 1.0 / jnp.sqrt(power / full_width + EPSILON)
    q_out[...] = inverse[:, :slots]
    lane = lax.broadcasted_iota(jnp.int32, (1, HD), 1)
    valid = tag_ref[1].astype(F32)
    segment = tag_ref[2].astype(F32)
    tags = jnp.where(lane == 0, valid, jnp.where(lane == 1, segment, 0.0))
    for device in range(note_out.shape[0]):
        note_out[device, :, :slots] = inverse[:, slots:]
        note_out[device, :, slots:] = tags


def head_kernel(
    first, last, total_heads, skip, tag_ref, notes, q_inverse, gain_q_ref, gain_k_ref, q_ref, g_ref,
    own_ref, near_ref, side_ref, swap_ref, *rest,
):
    state_in = rest[0] if first else None
    q_out, own_out, near_out, side_out, swap_out, state_out, *rows_out = rest[skip:-6]
    score_ref, grad_ref, weight_low, grad_low, inverse_ref, inner_ref = rest[-6:]
    step = pl.program_id(0)
    slots = q_ref.shape[1]
    width = total_heads * HD
    scale = 1.0 / math.sqrt(HD)
    steep = scale / math.log(2.0)
    mine = tag_ref[0]
    even = lax.rem(mine, 2) == 0
    distances = (0, 2, jnp.where(even, 3, 1), jnp.where(even, 1, 3))
    gain_q = gain_q_ref[...]
    gain_k = gain_k_ref[...]
    segment = tag_ref[2].astype(F32)
    others = [jnp.maximum(mine - distance, 0) for distance in distances]

    @pl.when(step == 0)
    def _():
        for slot in range(4):
            inverse_ref[slot] = along_lanes(notes[others[slot], :, :slots], HD)
        inverse_ref[4] = along_lanes(q_inverse[...], HD)
        inner_ref[...] = jnp.zeros_like(inner_ref)
        if first:
            state_out[...] = state_in[...]
        else:
            state_out[...] = jnp.zeros_like(state_out)

    q_unit = q_ref[0].astype(F32) * inverse_ref[4]
    q_norm = (q_unit * gain_q).astype(LOW)
    live = lax.broadcasted_iota(jnp.int32, (slots, HD), 0) < tag_ref[1]
    g_live = jnp.where(live, g_ref[0].astype(F32), 0.0).astype(LOW)
    q_side = jnp.transpose(q_norm)
    g_side = jnp.transpose(g_live)
    lanes = lax.broadcasted_iota(jnp.int32, (STRIP, slots), 0).astype(F32)
    refs = (own_ref, near_ref, side_ref, swap_ref)
    k_norms, limits = [], []
    for slot, ref in enumerate(refs):
        tags = notes[others[slot], :, slots:]
        same = (tags[:, 1:2] == segment) & (mine >= distances[slot])
        limits.append(jnp.where(same, tags[:, 0:1], 0.0))
        k_norm = (ref[:slots, :].astype(F32) * inverse_ref[slot] * gain_k).astype(LOW)
        k_norms.append(k_norm)
        rows = slice(slot * slots, (slot + 1) * slots)
        score_ref[rows, :] = jnp.dot(k_norm, q_side, preferred_element_type=F32)
        grad_ref[rows, :] = jnp.dot(ref[slots:, :], g_side, preferred_element_type=F32)
    strips = [(slot, at) for slot in range(4) for at in range(0, slots, STRIP)]
    top = jnp.full((8, slots), MASKED, F32)
    for slot, at in strips:
        base = slot * slots + at
        included = lanes < limits[slot] - at
        score = jnp.where(included, score_ref[base : base + STRIP, :], MASKED)
        top = jnp.maximum(top, folded(score, jnp.maximum))
    top = jnp.max(top, axis=0, keepdims=True)
    total = jnp.zeros((8, slots), F32)
    delta = jnp.zeros((8, slots), F32)
    for slot, at in strips:
        base = slot * slots + at
        included = lanes < limits[slot] - at
        score = jnp.where(included, score_ref[base : base + STRIP, :], MASKED)
        exponent = jnp.exp2((score - top) * steep)
        score_ref[base : base + STRIP, :] = exponent
        total += folded(exponent, jnp.add)
        delta += folded(exponent * grad_ref[base : base + STRIP, :], jnp.add)
    inverse_sum = 1.0 / jnp.sum(total, axis=0, keepdims=True)
    delta = jnp.sum(delta, axis=0, keepdims=True) * inverse_sum
    q_turned = jnp.zeros((HD, slots), F32)
    k_gain = jnp.zeros((1, HD), F32)
    for slot, out in enumerate((own_out, near_out, side_out, swap_out)):
        for at in range(0, slots, STRIP):
            rows = slice(slot * slots + at, slot * slots + at + STRIP)
            weight = score_ref[rows, :] * inverse_sum
            weight_low[rows, :] = weight.astype(LOW)
            grad_low[rows, :] = (weight * (grad_ref[rows, :] - delta)).astype(LOW)
        rows = slice(slot * slots, (slot + 1) * slots)
        q_turned += jnp.dot(
            jnp.transpose(k_norms[slot]), grad_low[rows, :], preferred_element_type=F32
        )
        k_part = jnp.dot(grad_low[rows, :], q_norm, preferred_element_type=F32) * scale
        v_part = jnp.dot(weight_low[rows, :], g_live, preferred_element_type=F32)
        out[:slots, :] = k_part.astype(out.dtype)
        out[slots:, :] = v_part.astype(out.dtype)
        product = k_part * (refs[slot][:slots, :].astype(F32) * inverse_ref[slot])
        k_gain += jnp.sum(product, axis=0, keepdims=True)
        inner_ref[slot] += product * gain_k
    q_part = jnp.transpose(q_turned) * scale
    q_out[...] = q_part
    product = q_part * q_unit
    inner_ref[4] += product * gain_q
    at = (first + step) * HD
    state_out[5:6, pl.ds(pl.multiple_of(at, HD), HD)] = jnp.sum(product, axis=0, keepdims=True)
    state_out[5:6, pl.ds(pl.multiple_of(width + at, HD), HD)] = k_gain

    @pl.when(step == last - first - 1)
    def _():
        for slot in range(5):
            state_out[slot : slot + 1, :slots] += row_sums(inner_ref[slot])
        if last == total_heads:
            (rows_ref,) = rows_out
            for device in range(rows_ref.shape[0]):
                rows_ref[device, :, :slots] = jnp.zeros((1, slots), F32)
                rows_ref[device, :, slots:] = state_out[5:6, :]
            for slot, distance in enumerate(distances):
                @pl.when(mine >= distance)
                def _():
                    rows_ref[mine - distance, :, :slots] = state_out[slot : slot + 1, :slots]


def head_blocks(first, rows):
    return pl.BlockSpec((rows, HD), lambda head: (0, first + head))


def raw_blocks(first, slots):
    return pl.BlockSpec((1, slots, HD), lambda head: (0, 0, first + head))


def all_of(shape):
    return pl.BlockSpec(shape, lambda *_: (0,) * len(shape))


def attend(
    first, last, chunk, heads, groups, tags, notes, q_inverse, gain_q, gain_k, q, g, halo, state, outs
):
    slots = q.shape[1]
    width = (chunk[1] - chunk[0]) * HD
    place = first - chunk[0]
    state_shape = (8, 2 * heads * HD)
    row_shape = (groups, 1, slots + 2 * heads * HD)
    final = last == heads
    known = 11 + len(state)
    return pl.pallas_call(
        functools.partial(head_kernel, first, last, heads, len(state) + len(outs)),
        grid=(last - first,),
        in_specs=[
            pl.BlockSpec(memory_space=pltpu.SMEM),
            all_of(notes.shape),
            all_of((1, slots)),
            head_blocks(first, 1),
            head_blocks(first, 1),
            raw_blocks(first, slots),
            raw_blocks(first, slots),
            *[head_blocks(first, 2 * slots)] * 4,
            *[all_of(state_shape)] * len(state),
            *[pl.BlockSpec(memory_space=pl.ANY)] * len(outs),
        ],
        out_specs=[
            head_blocks(place, slots),
            *[head_blocks(place, 2 * slots)] * 4,
            all_of(state_shape),
            *[all_of(row_shape)] * final,
        ],
        out_shape=[
            struct((slots, width)),
            struct((2 * slots, width)),
            *[struct((2 * slots, width), LOW)] * 3,
            struct(state_shape),
            *[struct(row_shape)] * final,
        ],
        scratch_shapes=[
            pltpu.VMEM((4 * slots, slots), F32),
            pltpu.VMEM((4 * slots, slots), F32),
            pltpu.VMEM((4 * slots, slots), LOW),
            pltpu.VMEM((4 * slots, slots), LOW),
            pltpu.VMEM((5, slots, HD), F32),
            pltpu.VMEM((5, slots, HD), F32),
        ],
        input_output_aliases={known + i: i for i in range(len(outs))},
        compiler_params=kernel_params(),
        cost_estimate=pl.CostEstimate(
            flops=(last - first) * 40 * slots * slots * HD,
            bytes_accessed=(last - first) * 44 * slots * HD,
            transcendentals=(last - first) * 4 * slots * slots,
        ),
    )(tags, notes, q_inverse, gain_q, gain_k, q, g, *halo, *state, *outs)


def collect_kernel(state_ref, rows_ref, inner_out, gain_out):
    slots = inner_out.shape[2] // 2
    total = rows_ref[0]
    for device in range(1, rows_ref.shape[0]):
        total += rows_ref[device]
    for device in range(inner_out.shape[0]):
        inner_out[device, :, :slots] = state_ref[4:5, :slots]
        inner_out[device, :, slots:] = total[:, :slots]
    for device in range(gain_out.shape[0]):
        gain_out[device] = total[:, slots:]


def total_of(sums):
    total = sums[0]
    for other in range(1, sums.shape[0]):
        total += sums[other]
    return total


def query_kernel(
    full_width, q_inverse, gain_ref, inners, q_ref, q_part, query_out, turned
):
    rows, width = q_ref.shape[1:]
    slots = q_inverse.shape[1]
    step = pl.program_id(0)

    @pl.when(step == 0)
    def _():
        inner = total_of(inners)[:, :slots] / full_width
        turned[0] = along_lanes(q_inverse[...], HD)
        turned[1] = along_lanes(inner, HD) * turned[0]

    here = pl.ds(pl.multiple_of(step * rows, 16), rows)
    inverse, inner = turned[0, here, :], turned[1, here, :]
    for at in range(0, width, HD):
        lanes = slice(at, at + HD)
        scaled = q_part[:, lanes] * gain_ref[:, lanes]
        query_out[0, :, lanes] = ((scaled - q_ref[0, :, lanes].astype(F32) * inner) * inverse).astype(LOW)


def key_kernel(
    full_width, tag_ref, notes, gain_ref, inners, k_ref, k_own, v_own, k_side, v_side, k_near,
    v_near, key_out, value_out, turned,
):
    rows, width = k_ref.shape[1:]
    slots = turned.shape[1]
    mine = tag_ref[0]
    step = pl.program_id(0)

    @pl.when(step == 0)
    def _():
        inner = total_of(inners)[:, slots:] / full_width
        turned[0] = along_lanes(notes[mine, :, :slots], HD)
        turned[1] = along_lanes(inner, HD) * turned[0]

    here = pl.ds(pl.multiple_of(step * rows, 16), rows)
    inverse, inner = turned[0, here, :], turned[1, here, :]
    keep = jnp.where(lax.rem(mine, 2) == 0, 1.0, 0.0)
    for at in range(0, width, HD):
        lanes = slice(at, at + HD)
        total = k_own[:, lanes] + k_near[:, lanes].astype(F32)
        total += k_side[:, lanes].astype(F32) * keep
        scaled = total * gain_ref[:, lanes]
        key_out[0, :, lanes] = ((scaled - k_ref[0, :, lanes].astype(F32) * inner) * inverse).astype(LOW)
        total = v_own[:, lanes] + v_near[:, lanes].astype(F32)
        value_out[0, :, lanes] = (total + v_side[:, lanes].astype(F32) * keep).astype(LOW)


def struct(shape, dtype=F32):
    return jax.ShapeDtypeStruct(shape, dtype)


def kernel_params(limit=VMEM_LIMIT):
    return pltpu.CompilerParams(vmem_limit_bytes=limit)


def on_device(q_proj, k_proj, values, grad_out, gain_q, gain_k, valid_count, segment):
    _, slots, local_width = q_proj.shape
    heads = local_width // HD
    mp_size, dp_size = lax.axis_size("mp"), lax.axis_size("dp")
    full_width = local_width * mp_size
    groups = lax.axis_size("tm")
    mine = lax.axis_index("tm")
    even = mine % 2 == 0
    tags = jnp.stack([mine, valid_count[0, 0], segment[0, 0]]).astype(jnp.int32)
    gain_q = gain_q.reshape(1, local_width)
    gain_k = gain_k.reshape(1, local_width)
    smem = pl.BlockSpec(memory_space=pltpu.SMEM)

    two_on = [(i, i + 2) for i in range(groups - 2)]
    one_on = [(i, i + 1) for i in range(groups - 1)]
    pair = [(i, i ^ 1) for i in range(groups)]
    back = lambda moves: [(there, here) for here, there in moves]

    anywhere = pl.BlockSpec(memory_space=pl.ANY)
    own = jnp.concatenate([k_proj[0], values[0]], axis=0)
    near = lax.ppermute(own, "tm", two_on)
    power = pl.pallas_call(
        power_kernel,
        out_shape=struct((mp_size, 1, 2 * slots)),
        compiler_params=kernel_params(),
        cost_estimate=pl.CostEstimate(flops=10**6, bytes_accessed=10**6, transcendentals=0),
    )(q_proj, k_proj)
    powers = lax.all_to_all(power, "mp", 0, 0, tiled=True)
    note, q_inverse = pl.pallas_call(
        functools.partial(roots_kernel, full_width),
        in_specs=[smem, pl.BlockSpec()],
        out_shape=[struct((groups, 1, slots + HD)), struct((1, slots))],
        compiler_params=kernel_params(),
    )(tags, powers)
    near, note = lax.optimization_barrier((near, note))
    passed, note = lax.optimization_barrier((jnp.where(even, own, near), note))
    side = lax.ppermute(passed, "tm", one_on)
    swap = lax.ppermute(near, "tm", pair)
    notes = lax.all_to_all(note, "tm", 0, 0, tiled=True)

    q_part, own_part, near_part, side_part, swap_part, state, rows = attend(
        0, heads, (0, heads), heads, groups, tags, notes, q_inverse, gain_q, gain_k, q_proj,
        grad_out, (own, near, side, swap), [], [],
    )
    side_back = lax.ppermute(side_part, "tm", back(one_on))
    swap_back = lax.ppermute(swap_part, "tm", pair)
    rows = lax.all_to_all(rows, "tm", 0, 0, tiled=True)
    inners, gains = pl.pallas_call(
        collect_kernel,
        out_shape=[struct((mp_size, 1, 2 * slots)), struct((dp_size, 1, 2 * local_width))],
        compiler_params=kernel_params(),
    )(state, rows)
    near_sum = near_part.astype(F32) + swap_back.astype(F32)
    near_sum = (near_sum + jnp.where(even, 0.0, side_back.astype(F32))).astype(LOW)
    inners, near_sum = lax.optimization_barrier((inners, near_sum))
    near_back = lax.ppermute(near_sum, "tm", back(two_on))
    inners = lax.all_to_all(inners, "mp", 0, 0, tiled=True)
    gains, inners = lax.optimization_barrier((gains, inners))
    gains = lax.all_to_all(gains, "dp", 0, 0, tiled=True)

    steps = 4
    block = slots // steps
    raw = pl.BlockSpec((1, block, local_width), lambda step: (0, step, 0))
    upper = pl.BlockSpec((block, local_width), lambda step: (step, 0))
    lower = pl.BlockSpec((block, local_width), lambda step: (step + steps, 0))
    query_grad = pl.pallas_call(
        functools.partial(query_kernel, full_width),
        grid=(steps,),
        in_specs=[
            all_of((1, slots)),
            all_of((1, local_width)),
            all_of(inners.shape),
            raw,
            upper,
        ],
        out_specs=raw,
        out_shape=struct(q_proj.shape, LOW),
        scratch_shapes=[pltpu.VMEM((2, slots, HD), F32)],
        compiler_params=kernel_params(),
        cost_estimate=pl.CostEstimate(flops=10**6, bytes_accessed=3 * 10**6, transcendentals=0),
    )(q_inverse, gain_q, inners, q_proj, q_part)
    key_grad, value_grad = pl.pallas_call(
        functools.partial(key_kernel, full_width),
        grid=(steps,),
        in_specs=[
            smem,
            all_of(notes.shape),
            all_of((1, local_width)),
            all_of(inners.shape),
            raw,
            *[upper, lower] * 3,
        ],
        out_specs=[raw] * 2,
        out_shape=[struct(q_proj.shape, LOW)] * 2,
        scratch_shapes=[pltpu.VMEM((2, slots, HD), F32)],
        compiler_params=kernel_params(16 * 1024 * 1024),
        cost_estimate=pl.CostEstimate(flops=10**6, bytes_accessed=5 * 10**6, transcendentals=0),
    )(
        tags, notes, gain_k, inners, k_proj,
        own_part, own_part, side_back, side_back, near_back, near_back,
    )
    gains, key_grad = lax.optimization_barrier((gains, key_grad))
    gain_sum = jnp.sum(gains[:, 0], axis=0)
    return query_grad, key_grad, value_grad, gain_sum[:local_width], gain_sum[local_width:]


def solution(mesh):
    wide = P("dp", "tm", "mp")
    in_specs = (wide, wide, wide, wide, P("mp"), P("mp"), P("dp", "tm"), P("dp", "tm"))
    out_specs = (wide, wide, wide, P("mp"), P("mp"))
    return jax.shard_map(
        on_device, mesh=mesh, in_specs=in_specs, out_specs=out_specs, check_vma=False
    )
```
